512 devices in a mesh: row: 16 (over z, y_hi), col: 32 (over x, y_lo, core).
Axes of the slice: x: 4, y: 8 (y_hi: 2, y_lo: 4; y = y_hi * 4 + y_lo), z: 8, core: 2. Of those that a mesh axis runs over, the one named last changes fastest.
Arguments:
- tokens: bfloat16 [384, 12288], P('col', 'row'), may hold values from -6 to 6
- up_weight: bfloat16 [12288, 49152], P('row', 'col'), may hold values from -0.0546875 to 0.0546875
- up_bias: float32 [49152], P('col'), may hold values from -3 to 3
- down_weight: bfloat16 [49152, 12288], P('col', 'row'), may hold values from -0.02734375 to 0.02734375
- down_bias: float32 [12288], P('row'), may hold values from -3 to 3
Outputs:
- layer_out: bfloat16 [384, 12288], P('col', 'row')
The draws below stay inside these ranges and needn't reach their ends.
All inputs are finite; a program needn't handle non-finite values.
Results may differ from the reference program's by a relative error of at most 0.0034.
Values may be sent and summed in bfloat16 or wider, within the bound.
No kernel may reach another device: no remote copies, remote signals or barrier semaphores. Data moves between devices by JAX's collectives and lax.ppermute only.
A program may use at most 64 MiB of HBM per device.

```python
import jax
import jax.numpy as jnp

D = 12288
FF = 49152
TOKENS = 384


def levels(key, shape, shards, smallest, largest):
    gain = 1.0
    for axis_at, blocks in shards:
        steps = jax.random.uniform(jax.random.fold_in(jax.random.fold_in(key, 6), axis_at), (blocks,), jnp.float32, smallest / len(shards), largest / len(shards))
        gain = gain * jnp.repeat(jnp.exp(steps), shape[axis_at] // blocks).reshape((-1,) + (1,) * (len(shape) - 1 - axis_at))
    return gain


def noise(own_key, dims, deviation, reach, shards=(), held_as=jnp.bfloat16):
    result = jax.random.normal(own_key, dims, jnp.float32) * deviation
    if len(shards) > 0:
        result = levels(own_key, dims, shards, -0.22, 0.18) * result
    return jnp.clip(result, min=-reach, max=reach).astype(held_as)


def setup_inputs(seed: int = 0) -> dict:
    key_list = jax.random.split(jax.random.key(seed), 6)
    tokens = noise(key_list[0], (TOKENS, D), 1.0, 6.0, ((0, 32), (1, 16)))
    up_weight = noise(key_list[1], (D, FF), D ** -0.5, 0.0546875, ((0, 16), (1, 32)))
    up_bias = noise(key_list[2], (FF,), 0.5, 3.0, ((0, 32),), jnp.float32)
    down_weight = noise(key_list[3], (FF, D), FF ** -0.5, 0.02734375, ((0, 32), (1, 16)))
    down_bias = noise(key_list[4], (D,), 0.5, 3.0, ((0, 16),), jnp.float32)
    return dict(tokens=tokens, up_weight=up_weight, up_bias=up_bias, down_weight=down_weight, down_bias=down_bias)


def reference(tokens, up_weight, up_bias, down_weight, down_bias):
    pre_act = jnp.dot(tokens, up_weight, preferred_element_type=jnp.float32) + up_bias
    activated = jax.nn.gelu(pre_act, approximate=True).astype(jnp.bfloat16)
    branch = jnp.dot(activated, down_weight, preferred_element_type=jnp.float32)
    return (tokens.astype(jnp.float32) + branch + down_bias).astype(jnp.bfloat16)
```

```python
import jax
import jax.numpy as jnp
from jax import lax
from jax.sharding import Mesh, PartitionSpec as P

AXES = {"z": 8, "h": 2, "x": 4, "y": 4, "c": 2}
ROW = ("z", "h")
COL = ("x", "y", "c")


def swap(value, axis):
    return lax.ppermute(value, axis, [(0, 1), (1, 0)])


def spread(value, axes, members):
    copies = jnp.broadcast_to(value, (members,) + value.shape)
    return lax.all_to_all(copies, axes, 0, 0)


def on_device(tokens, up_weight, up_bias, down_weight, down_bias):
    bf16, f32 = jnp.bfloat16, jnp.float32
    own, width = tokens.shape
    up_other = swap(up_weight, "c")
    bias_other = swap(up_bias, "c")
    down_other = swap(down_weight, "c")

    plane = spread(tokens, ("x", "y"), 16).reshape(16 * own, width)
    partial_up = jnp.concatenate(
        [
            jnp.dot(plane, up_weight, preferred_element_type=f32).astype(bf16),
            jnp.dot(plane, up_other, preferred_element_type=f32).astype(bf16),
        ],
        axis=1,
    )
    hidden = partial_up.shape[1]
    along_z = lax.all_to_all(partial_up.reshape(8, 2 * own, hidden), "z", 0, 0)
    summed_z = jnp.sum(along_z.astype(f32), axis=0)
    summed_up = summed_z + swap(summed_z.astype(bf16), "h").astype(f32)
    bias = jnp.concatenate([up_bias, bias_other])
    activated = jax.nn.gelu(summed_up + bias, approximate=True).astype(bf16)

    gathered = spread(activated, "z", 8).reshape(16 * own, hidden)
    half = hidden // 2
    partial_down = jnp.dot(gathered[:, :half], down_weight, preferred_element_type=f32) + jnp.dot(
        gathered[:, half:], down_other, preferred_element_type=f32
    )
    parts = lax.all_to_all(partial_down.astype(bf16).reshape(16, own, width), ("x", "y"), 0, 0)
    branch = jnp.sum(parts.astype(f32), axis=0)
    return (tokens.astype(f32) + branch + down_bias).astype(bf16)


def solution(mesh):
    fine = Mesh(mesh.devices.reshape(tuple(AXES.values())), tuple(AXES))
    placed = (P(COL, ROW), P(ROW, COL), P(COL), P(COL, ROW), P(ROW))
    return jax.shard_map(
        on_device, mesh=fine, in_specs=placed, out_specs=P(COL, ROW), check_vma=False
    )
```

```python
import jax
import jax.numpy as jnp
from jax import lax
from jax.sharding import Mesh, PartitionSpec as P

AXES = {"q": 4, "p": 2, "h": 2, "x": 4, "y": 4, "c": 2}
ROW = ("q", "p", "h")
COL = ("x", "y", "c")


def swap(value, axis):
    return lax.ppermute(value, axis, [(0, 1), (1, 0)])


def trade(value):
    def other(z, c):
        return (((z - c) % 8 ^ 1) + c) % 8

    pairs = [(z * 2 + c, other(z, c) * 2 + c) for z in range(8) for c in range(2)]
    return lax.ppermute(value, ("q", "p", "c"), pairs)


def tie(*values):
    tied = lax.optimization_barrier(values)
    return tied if len(values) > 1 else tied[0]


def spread(value, axes, members):
    copies = jnp.broadcast_to(value, (members,) + value.shape)
    return lax.all_to_all(copies, axes, 0, 0)


def on_device(tokens, up_weight, up_bias, down_weight, down_bias):
    bf16, f32 = jnp.bfloat16, jnp.float32
    own, width = tokens.shape
    even = lax.axis_index("p") == 0

    def keep_and_send(mine):
        other = swap(mine, "c")
        return jnp.where(even, mine, other), jnp.where(even, other, mine)

    gathered = spread(tokens, ("x", "y"), 16)
    up_keep, up_send = tie(*keep_and_send(up_weight))
    bias_keep, _ = keep_and_send(up_bias)
    down_keep, down_send = tie(*keep_and_send(down_weight))

    plane = gathered.reshape(16 * own, width)
    sent = jnp.dot(plane, up_send, preferred_element_type=f32).astype(bf16)
    kept = tie(jnp.dot(plane, up_keep, preferred_element_type=f32))
    pair_sum = (kept + trade(sent).astype(f32)).astype(bf16)
    parts_up = lax.all_to_all(pair_sum.reshape(4, 4 * own, -1), "q", 0, 0)
    summed_z = jnp.sum(parts_up.astype(f32), axis=0)
    halves = lax.all_gather(summed_z.astype(bf16), "h", axis=0)
    summed_up = summed_z + jnp.where(lax.axis_index("h") == 0, halves[1], halves[0]).astype(f32)
    activated = jax.nn.gelu(summed_up + bias_keep, approximate=True).astype(bf16)

    held = lax.all_gather(activated, "q", axis=0, tiled=True)
    partial_down = tie(jnp.dot(held, down_keep, preferred_element_type=f32)) + jnp.dot(
        trade(held), down_send, preferred_element_type=f32
    )
    parts = lax.all_to_all(partial_down.astype(bf16).reshape(16, own, width), ("x", "y"), 0, 0)
    branch = jnp.sum(parts.astype(f32), axis=0)
    return (tokens.astype(f32) + branch + down_bias).astype(bf16)


def solution(mesh):
    fine = Mesh(mesh.devices.reshape(tuple(AXES.values())), tuple(AXES))
    placed = (P(COL, ROW), P(ROW, COL), P(COL), P(COL, ROW), P(ROW))
    return jax.shard_map(
        on_device, mesh=fine, in_specs=placed, out_specs=P(COL, ROW), check_vma=False
    )
```

```python
import jax
import jax.numpy as jnp
from jax import lax
from jax.sharding import Mesh, PartitionSpec as P

AXES = {"q": 4, "p": 2, "h": 2, "x": 4, "y": 4, "c": 2}
ROW = ("q", "p", "h")
COL = ("x", "y", "c")


def swap(value, axis):
    return lax.ppermute(value, axis, [(0, 1), (1, 0)])


def trade(value):
    def other(z, c):
        return (((z - c) % 8 ^ 1) + c) % 8

    pairs = [(z * 2 + c, other(z, c) * 2 + c) for z in range(8) for c in range(2)]
    return lax.ppermute(value, ("q", "p", "c"), pairs)


FIRST = 10
PLANE = [[(k + FIRST) % 16 * 2 + c for k in range(16)] for c in range(2)]


def in_plane(members):
    return lax.all_to_all(members, COL, 0, 0, axis_index_groups=PLANE)


def tie(*values):
    tied = lax.optimization_barrier(values)
    return tied if len(values) > 1 else tied[0]


def on_device(tokens, up_weight, up_bias, down_weight, down_bias):
    bf16, f32 = jnp.bfloat16, jnp.float32
    own, width = tokens.shape
    even = lax.axis_index("p") == 0

    def keep_and_send(mine):
        other = swap(mine, "c")
        return jnp.where(even, mine, other), jnp.where(even, other, mine)

    gathered = in_plane(jnp.broadcast_to(tokens, (16, own, width)))
    up_keep, up_send = tie(*keep_and_send(up_weight))
    bias_keep, _ = keep_and_send(up_bias)
    down_keep, down_send = tie(*keep_and_send(down_weight))

    plane = gathered.reshape(16 * own, width)
    sent = jnp.dot(plane, up_send, preferred_element_type=f32).astype(bf16)
    kept = tie(jnp.dot(plane, up_keep, preferred_element_type=f32))
    pair_sum = (kept + trade(sent).astype(f32)).astype(bf16)
    parts_up = lax.all_to_all(pair_sum.reshape(4, 4 * own, -1), "q", 0, 0)
    summed_z = jnp.sum(parts_up.astype(f32), axis=0)
    halves = lax.all_gather(summed_z.astype(bf16), "h", axis=0)
    summed_up = summed_z + jnp.where(lax.axis_index("h") == 0, halves[1], halves[0]).astype(f32)
    activated = jax.nn.gelu(summed_up + bias_keep, approximate=True).astype(bf16)

    held = lax.all_gather(activated, "q", axis=0, tiled=True)
    partial_down = tie(jnp.dot(held, down_keep, preferred_element_type=f32)) + jnp.dot(
        trade(held), down_send, preferred_element_type=f32
    )
    parts = in_plane(partial_down.astype(bf16).reshape(16, own, width))
    branch = jnp.sum(parts.astype(f32), axis=0)
    return (tokens.astype(f32) + branch + down_bias).astype(bf16)


def solution(mesh):
    fine = Mesh(mesh.devices.reshape(tuple(AXES.values())), tuple(AXES))
    placed = (P(COL, ROW), P(ROW, COL), P(COL), P(COL, ROW), P(ROW))
    return jax.shard_map(
        on_device, mesh=fine, in_specs=placed, out_specs=P(COL, ROW), check_vma=False
    )
```

```python
import jax
import jax.numpy as jnp
from jax import lax
from jax.sharding import Mesh, PartitionSpec as P

AXES = {"q": 4, "p": 2, "h": 2, "x": 4, "y": 4, "c": 2}
ROW = ("q", "p", "h")
COL = ("x", "y", "c")


def swap(value, axis):
    return lax.ppermute(value, axis, [(0, 1), (1, 0)])


def trade(value):
    def other(z, c):
        return (((z - c) % 8 ^ 1) + c) % 8

    pairs = [(z * 2 + c, other(z, c) * 2 + c) for z in range(8) for c in range(2)]
    return lax.ppermute(value, ("q", "p", "c"), pairs)


FIRST = 10
PLANE = [[((k + FIRST) % 4 * 4 + (k + FIRST) // 4 % 4) * 2 + c for k in range(16)] for c in range(2)]


def in_plane(members):
    return lax.all_to_all(members, COL, 0, 0, axis_index_groups=PLANE)


def tie(*values):
    tied = lax.optimization_barrier(values)
    return tied if len(values) > 1 else tied[0]


def on_device(tokens, up_weight, up_bias, down_weight, down_bias):
    bf16, f32 = jnp.bfloat16, jnp.float32
    own, width = tokens.shape
    even = lax.axis_index("p") == 0

    def keep_and_send(mine):
        other = swap(mine, "c")
        return jnp.where(even, mine, other), jnp.where(even, other, mine)

    gathered = in_plane(jnp.broadcast_to(tokens, (16, own, width)))
    up_keep, up_send = tie(*keep_and_send(up_weight))
    bias_keep, _ = keep_and_send(up_bias)
    down_keep, down_send = tie(*keep_and_send(down_weight))

    plane = gathered.reshape(16 * own, width)
    sent = jnp.dot(plane, up_send, preferred_element_type=f32).astype(bf16)
    kept = tie(jnp.dot(plane, up_keep, preferred_element_type=f32))
    pair_sum = (kept + trade(sent).astype(f32)).astype(bf16)
    parts_up = lax.all_to_all(pair_sum.reshape(4, 4 * own, -1), "q", 0, 0)
    summed_z = jnp.sum(parts_up.astype(f32), axis=0)
    halves = lax.all_gather(summed_z.astype(bf16), "h", axis=0)
    summed_up = summed_z + jnp.where(lax.axis_index("h") == 0, halves[1], halves[0]).astype(f32)
    activated = jax.nn.gelu(summed_up + bias_keep, approximate=True).astype(bf16)

    held = lax.all_gather(activated, "q", axis=0, tiled=True)
    partial_down = tie(jnp.dot(held, down_keep, preferred_element_type=f32)) + jnp.dot(
        trade(held), down_send, preferred_element_type=f32
    )
    parts = in_plane(partial_down.astype(bf16).reshape(16, own, width))
    branch = jnp.sum(parts.astype(f32), axis=0)
    return (tokens.astype(f32) + branch + down_bias).astype(bf16)


def solution(mesh):
    fine = Mesh(mesh.devices.reshape(tuple(AXES.values())), tuple(AXES))
    placed = (P(COL, ROW), P(ROW, COL), P(COL), P(COL, ROW), P(ROW))
    return jax.shard_map(
        on_device, mesh=fine, in_specs=placed, out_specs=P(COL, ROW), check_vma=False
    )
```
